1024 devices in a mesh: expert: 64 (over z, core), tensor: 16 (over y, x).
Axes of the slice: x: 4, y: 4, z: 32, core: 2. Of those that a mesh axis runs over, the one named last changes fastest.
Arguments:
- tokens: bfloat16 [1536, 4096], P('expert', 'tensor'), may hold values from -6 to 6
- routes: int32 [1536, 8], P('expert'), may hold values from 0 to 63, all different within a row; in each aligned block of 24 rows (0 to 23, 24 to 47, ...) at most 4 rows name the same one
- gates: float32 [1536, 8], P('expert'), may hold values from 0.1 to 1
- cotangent: bfloat16 [1536, 4096], P('expert', 'tensor'), may hold values from -6 to 6
- w_gate: bfloat16 [64, 768, 4096], P('expert', 'tensor'), may hold values from -0.09375 to 0.09375
- w_up: bfloat16 [64, 768, 4096], P('expert', 'tensor'), may hold values from -0.09375 to 0.09375
- w_down: bfloat16 [64, 768, 4096], P('expert', 'tensor'), may hold values from -0.21875 to 0.21875
Outputs:
- mixed: bfloat16 [1536, 4096], P('expert', 'tensor')
- token_grad: bfloat16 [1536, 4096], P('expert', 'tensor')
- gate_grad: bfloat16 [64, 768, 4096], P('expert', 'tensor')
- up_grad: bfloat16 [64, 768, 4096], P('expert', 'tensor')
- down_grad: bfloat16 [64, 768, 4096], P('expert', 'tensor')
The draws below stay inside these ranges and needn't reach their ends.
Inputs may be any that keep to these rules, and one draw needn't show every extreme that they name: `routes`: each row names 8 different experts. Among the 24 rows of one index of the expert axis, no expert is named by more than 4 rows, a bound that some block reaches.
All inputs are finite; a program needn't handle non-finite values.
Results may differ from the reference program's by a relative error of at most 0.02.
Values may be sent and summed in bfloat16 or wider, within the bound.
No kernel may reach another device: no remote copies, remote signals or barrier semaphores. Data moves between devices by JAX's collectives and lax.ppermute only.
A program may use at most 32 MiB of HBM per device.

```python
import math
import jax
import jax.numpy as jnp
import numpy as np
from jax import lax

D = 4096
FF = 768
TOP = 8
CAP = 4
EXPERTS = 64
TOK_DEV = 24
TOKENS = 1536
N_EXPERT = 64
N_TENSOR = 16


def levels(key, extent, cuts, least, largest):
    gain, own = 1.0, jax.random.fold_in(key, 6)
    for dim, blocks in cuts:
        draws = jnp.exp(jax.random.uniform(jax.random.fold_in(own, dim), (blocks,), jnp.float32, least / len(cuts), largest / len(cuts)))
        gain = gain * jnp.repeat(draws, extent[dim] // blocks).reshape([-1 if axis == dim else 1 for axis in range(len(extent))])
    return gain


def shared_out(rng, own, number, rows, amount, top, limit, skew):
    sequence = jax.random.permutation(rng, amount)
    crowded, usual = portions_of(amount, rows * top, limit, skew, True), portions_of(amount, rows * top, limit, skew, False)
    places = jnp.arange(amount)

    def named(tallies, offset_by):
        used = int((tallies > 0).sum())
        fixed = max(1, used // 4)
        shifted = fixed + (places - fixed + offset_by * (used - fixed)) % max(1, amount - fixed)
        return jnp.zeros((amount,), jnp.int32).at[sequence[jnp.where(places < fixed, places, shifted)]].set(jnp.asarray(tallies, jnp.int32))

    tallies = jnp.where(number % 4 == 0, named(crowded, number // 4), named(usual, number - number // 4 - 1))
    mixed = jax.random.permutation(jax.random.fold_in(own, 3), amount)
    source_of, taker = mixed[0:amount // 2 * 2:2], mixed[1:amount // 2 * 2:2]
    slack = jnp.minimum(tallies[source_of] - 1, limit - tallies[taker]) // 2
    slack = jnp.where((source_of == sequence[0]) | (taker == sequence[0]) | (tallies[taker] == 0), 0, jnp.maximum(slack, 0))
    shifted = jax.random.randint(jax.random.fold_in(own, 4), (amount // 2,), 0, 1 << 20) % (slack + 1)
    tallies = tallies.at[source_of].add(-shifted).at[taker].add(shifted)
    members = jnp.searchsorted(jnp.cumsum(tallies), jnp.arange(rows * top), side="right").astype(jnp.int32)
    listing = members.reshape(top, rows).T
    listing = listing[jax.random.permutation(jax.random.fold_in(own, 1), rows)]
    offset_by = jax.random.randint(jax.random.fold_in(own, 2), (rows, 1), 0, top)
    return jnp.take_along_axis(listing, (jnp.arange(top)[None, :] + offset_by) % top, axis=1)


def portions_of(amount, total, most, slope, full):
    portions = [(1 << 20) // math.isqrt(grade ** slope) + 1 for grade in range(1, amount + 1)]
    largest = most if full else min(most, max(-(-total // amount), total * portions[0] // sum(portions)))
    least = 1 if total - largest >= amount - 1 else 0
    given, surplus = [largest] + [least] * (amount - 1), total - largest - least * (amount - 1)
    while surplus > 0:
        movable = [i for i in range(1, amount) if given[i] < largest] or [i for i in range(1, amount) if given[i] < most]
        whole, remaining = sum([portions[i] for i in movable]), surplus
        for i in movable:
            extra = min(most - given[i], max(1, remaining * portions[i] // whole), surplus)
            given[i] = given[i] + extra
            surplus = surplus - extra
    return np.array(given)


def gaussian(stream_key, extent, deviation, limit, split=(), kind=jnp.bfloat16):
    result = jax.random.normal(stream_key, extent, jnp.float32) * deviation
    if len(split) > 0:
        result = levels(stream_key, extent, split, -0.22, 0.18) * result
    return jnp.clip(result, min=-limit, max=limit).astype(kind)


def setup_inputs(seed: int = 0) -> dict:
    splits = jax.random.split(jax.random.key(seed), 8)
    tokens = gaussian(splits[0], (TOKENS, D), 1.0, 6.0, ((0, 64), (1, 16)))
    routes_keys = jax.random.split(jax.random.fold_in(splits[1], 1), TOKENS // TOK_DEV)
    routes_turns = jax.random.permutation(jax.random.fold_in(splits[1], 3), TOKENS // TOK_DEV)
    routes = jax.vmap(lambda own, number: shared_out(jax.random.fold_in(splits[1], 2), own, number, TOK_DEV, EXPERTS, TOP, CAP, 2))(routes_keys, routes_turns).reshape((TOKENS, TOP))
    gates = jnp.clip(0.1 + 0.9 * jax.random.uniform(splits[2], (TOKENS, TOP), jnp.float32) ** levels(splits[2], (TOKENS, TOP), ((0, 64),), -0.2, 0.2), 0.1, 1.0)
    cotangent = gaussian(splits[3], (TOKENS, D), 1.0, 6.0, ((0, 64), (1, 16)))
    w_gate = gaussian(splits[4], (EXPERTS, FF, D), D ** -0.5, 0.09375, ((0, 64), (1, 16)))
    w_up = gaussian(splits[5], (EXPERTS, FF, D), D ** -0.5, 0.09375, ((0, 64), (1, 16)))
    w_down = gaussian(splits[6], (EXPERTS, FF, D), FF ** -0.5, 0.21875, ((0, 64), (1, 16)))
    return dict(tokens=tokens, routes=routes, gates=gates, cotangent=cotangent, w_gate=w_gate, w_up=w_up, w_down=w_down)


def silu_pair(values):
    sigmoid = jax.nn.sigmoid(values)
    return values * sigmoid, sigmoid * (1.0 + values * (1.0 - sigmoid))


def rounded_sum(pieces):
    narrow = lax.optimization_barrier(pieces.astype(jnp.bfloat16))
    return jnp.sum(narrow.astype(jnp.float32), axis=0)


def reference(tokens, routes, gates, cotangent, w_gate, w_up, w_down):
    per_expert = N_EXPERT * CAP
    shard_width = FF // N_TENSOR
    blocks = routes.reshape(N_EXPERT, TOK_DEV * TOP)
    labels = jnp.arange(EXPERTS, dtype=jnp.int32)
    onehot = (blocks[:, :, None] == labels[None, None, :]).astype(jnp.int32)
    earlier = jnp.cumsum(onehot, axis=1) - onehot
    position = jnp.sum(earlier * onehot, axis=2)
    sources = jnp.arange(N_EXPERT, dtype=jnp.int32)[:, None]
    target = (blocks * per_expert + sources * CAP + position).reshape(-1).astype(jnp.int32)
    owners = (jnp.arange(TOKENS * TOP, dtype=jnp.int32) // TOP).astype(jnp.int32)
    dispatched = jnp.zeros((EXPERTS * per_expert, D), jnp.bfloat16).at[target].set(tokens[owners])
    dispatched = dispatched.reshape(EXPERTS, per_expert, D)
    weighted = (gates.reshape(-1)[:, None] * cotangent[owners].astype(jnp.float32)).astype(jnp.bfloat16)
    incoming = jnp.zeros((EXPERTS * per_expert, D), jnp.bfloat16).at[target].set(weighted)
    incoming = incoming.reshape(EXPERTS, per_expert, D)

    def expert(operands):
        inputs, grad_rows, gate_w, up_w, down_w = operands
        gate_pre = jnp.dot(inputs, gate_w.T, preferred_element_type=jnp.float32)
        up_pre = jnp.dot(inputs, up_w.T, preferred_element_type=jnp.float32)
        active, slopes = silu_pair(gate_pre)
        hidden = (active * up_pre).astype(jnp.bfloat16)
        pieces = jnp.einsum("rsf,sfd->srd",
                            hidden.reshape(per_expert, N_TENSOR, shard_width).astype(jnp.float32),
                            down_w.reshape(N_TENSOR, shard_width, D).astype(jnp.float32),
                            precision=lax.Precision.HIGHEST)
        outputs = rounded_sum(pieces).astype(jnp.bfloat16)
        hidden_grad = jnp.dot(grad_rows, down_w.T, preferred_element_type=jnp.float32)
        down_grad = jnp.dot(hidden.T, grad_rows, preferred_element_type=jnp.float32).astype(jnp.bfloat16)
        gate_delta = (hidden_grad * up_pre * slopes).astype(jnp.bfloat16)
        up_delta = (hidden_grad * active).astype(jnp.bfloat16)
        gate_grad = jnp.dot(gate_delta.T, inputs, preferred_element_type=jnp.float32).astype(jnp.bfloat16)
        up_grad = jnp.dot(up_delta.T, inputs, preferred_element_type=jnp.float32).astype(jnp.bfloat16)
        back_pieces = jnp.einsum("rsf,sfd->srd",
                                 gate_delta.reshape(per_expert, N_TENSOR, shard_width).astype(jnp.float32),
                                 gate_w.reshape(N_TENSOR, shard_width, D).astype(jnp.float32),
                                 precision=lax.Precision.HIGHEST)
        back_pieces = back_pieces + jnp.einsum("rsf,sfd->srd",
                                               up_delta.reshape(per_expert, N_TENSOR, shard_width).astype(jnp.float32),
                                               up_w.reshape(N_TENSOR, shard_width, D).astype(jnp.float32),
                                               precision=lax.Precision.HIGHEST)
        backward = rounded_sum(back_pieces).astype(jnp.bfloat16)
        return outputs, backward, gate_grad, up_grad, down_grad

    outputs_all, backward_all, gate_grad, up_grad, down_grad = lax.map(
        expert, (dispatched, incoming, w_gate, w_up, w_down))
    weights = gates.reshape(TOKENS, TOP, 1)
    picked = outputs_all.reshape(-1, D)[target].astype(jnp.float32).reshape(TOKENS, TOP, D)
    mixed = jnp.sum(weights * picked, axis=1).astype(jnp.bfloat16)
    picked_back = backward_all.reshape(-1, D)[target].astype(jnp.float32).reshape(TOKENS, TOP, D)
    token_grad = jnp.sum(weights * picked_back, axis=1).astype(jnp.bfloat16)
    return mixed, token_grad, gate_grad, up_grad, down_grad
```

```python
import jax
import jax.numpy as jnp
from jax import lax
from jax.sharding import PartitionSpec as P

CAP = 4
F32, BF16 = jnp.float32, jnp.bfloat16


def exchange(values, axis):
    return lax.all_to_all(values, axis, split_axis=0, concat_axis=0, tiled=True)


def slot_weights(routes, gates, experts):
    count = routes.shape[0]
    column = lax.broadcasted_iota(jnp.int32, (1, 1, experts * 2 * CAP), 2)
    chosen = routes[:, :, None] == column // (2 * CAP)
    named = jnp.sum(chosen.astype(F32), axis=1)
    weight = jnp.sum(jnp.where(chosen, gates[:, :, None], 0.0), axis=1)
    row = lax.broadcasted_iota(jnp.int32, (count, count), 0)
    before = (lax.broadcasted_iota(jnp.int32, (count, count), 1) < row).astype(BF16)
    position = jnp.dot(before, named.astype(BF16), preferred_element_type=F32).astype(jnp.int32)
    place = column[0] % (2 * CAP)
    first = named * (position == place)
    second = named * (position + CAP == place) * weight
    return jnp.concatenate([first, second]), jnp.concatenate([first * weight, second])


def shards(tokens, routes, gates, cotangent, w_gate, w_up, w_down):
    experts, groups = lax.axis_size("expert"), lax.axis_size("tensor")
    count, width = tokens.shape
    hidden_units = w_gate.shape[1]
    rows = experts * CAP

    weights = jnp.concatenate([w_gate[0], w_up[0], w_down[0]]).reshape(3 * hidden_units, groups, width)
    weights = exchange(weights.transpose(1, 0, 2), "tensor")
    weights_in, weights_out = weights[:, : 2 * hidden_units], weights[:, 2 * hidden_units :]

    spread, blend = slot_weights(routes, gates, experts)
    sent = lax.dot_general(
        spread,
        jnp.concatenate([tokens, cotangent]).astype(F32),
        (((0,), (0,)), ((), ())),
        precision=lax.Precision.HIGHEST,
    ).astype(BF16)
    arrived = exchange(sent.reshape(experts, 2 * CAP, width), "expert")
    inputs = arrived[:, :CAP].reshape(rows, width)
    grad_rows = arrived[:, CAP:].reshape(rows, width)

    def product(a, b, pattern):
        return jnp.einsum(pattern, a, b, preferred_element_type=F32)

    partial = jnp.concatenate(
        [
            product(weights_in, inputs, "sfd,rd->sfr").astype(BF16),
            product(weights_out, grad_rows, "sfd,rd->sfr").astype(BF16),
        ],
        axis=1,
    )
    summed = jnp.sum(exchange(partial, "tensor").astype(F32), axis=0)
    gate_pre = summed[:hidden_units]
    up_pre = summed[hidden_units : 2 * hidden_units]
    hidden_grad = summed[2 * hidden_units :]
    sigmoid = jax.nn.sigmoid(gate_pre)
    active = gate_pre * sigmoid
    slope = sigmoid * (1.0 + gate_pre * (1.0 - sigmoid))
    mine = jnp.concatenate([hidden_grad * up_pre * slope, hidden_grad * active, active * up_pre]).astype(BF16)
    copies = lax.optimization_barrier(jnp.broadcast_to(mine[None], (groups,) + mine.shape))
    whole = exchange(copies, "tensor")
    deltas, hidden = whole[:, : 2 * hidden_units], whole[:, 2 * hidden_units :]

    expert_out = product(hidden, weights_out, "sfr,sfd->rd").astype(BF16)
    expert_back = product(deltas, weights_in, "sfr,sfd->rd").astype(BF16)
    returned = jnp.concatenate(
        [expert_out.reshape(experts, CAP, width), expert_back.reshape(experts, CAP, width)], axis=1
    )
    returned = exchange(returned, "expert").reshape(2 * rows, width)

    grads = jnp.concatenate(
        [
            product(deltas, inputs, "sfr,rd->sfd").astype(BF16),
            product(hidden, grad_rows, "sfr,rd->sfd").astype(BF16),
        ],
        axis=1,
    )
    grads = exchange(grads, "tensor").transpose(1, 0, 2).reshape(3 * hidden_units, groups * width)

    mixed = jnp.dot(blend, returned.astype(F32), precision=lax.Precision.HIGHEST).astype(BF16)
    return (
        mixed[:count],
        mixed[count:],
        grads[None, :hidden_units],
        grads[None, hidden_units : 2 * hidden_units],
        grads[None, 2 * hidden_units :],
    )


def solution(mesh):
    by_row, by_hidden = P("expert", "tensor"), P("expert", "tensor", None)
    return jax.shard_map(
        shards,
        mesh=mesh,
        in_specs=(by_row, P("expert", None), P("expert", None), by_row, by_hidden, by_hidden, by_hidden),
        out_specs=(by_row, by_row, by_hidden, by_hidden, by_hidden),
        check_vma=False,
    )
```

```python
import math

import jax
import jax.numpy as jnp
from jax import lax
from jax.sharding import Mesh, PartitionSpec as P

CAP = 4
F32, BF16 = jnp.float32, jnp.bfloat16


def exchange(values, axis):
    return lax.all_to_all(values, axis, split_axis=0, concat_axis=0, tiled=True)


def share(values, axis):
    copies = jnp.broadcast_to(values[None], (lax.axis_size(axis),) + values.shape)
    return exchange(lax.optimization_barrier(copies), axis)


def product(a, b, pattern):
    return jnp.einsum(pattern, a, b, preferred_element_type=F32)


def swap(block_for, axis):
    size, me = lax.axis_size(axis), lax.axis_index(axis)
    moved = [block_for(me)]
    for shift in range(1, size):
        pairs = [(m, (m + shift) % size) for m in range(size)]
        moved.append(lax.ppermute(block_for((me + shift) % size), axis, pairs))
    ordered = []
    for m in range(size):
        shift = (me - m) % size
        block = moved[0]
        for other in range(1, size):
            block = jnp.where(shift == other, moved[other], block)
        ordered.append(block)
    return ordered


def slot_weights(routes, gates, experts):
    count = routes.shape[0]
    column = lax.broadcasted_iota(jnp.int32, (1, 1, experts * 2 * CAP), 2)
    chosen = routes[:, :, None] == column // (2 * CAP)
    named = jnp.sum(chosen.astype(F32), axis=1)
    weight = jnp.sum(jnp.where(chosen, gates[:, :, None], 0.0), axis=1)
    row = lax.broadcasted_iota(jnp.int32, (count, count), 0)
    before = (lax.broadcasted_iota(jnp.int32, (count, count), 1) < row).astype(BF16)
    position = jnp.dot(before, named.astype(BF16), preferred_element_type=F32).astype(jnp.int32)
    place = column[0] % (2 * CAP)
    first = named * (position == place)
    second = named * (position + CAP == place) * weight
    return jnp.concatenate([first, second]), jnp.concatenate([first * weight, second])


def shards(tokens, routes, gates, cotangent, w_gate, w_up, w_down):
    experts, high, wide = lax.axis_size("expert"), lax.axis_size("row"), lax.axis_size("col")
    count, width = tokens.shape
    units = w_gate.shape[1]
    rows = experts * CAP

    spread, blend = slot_weights(routes, gates, experts)
    sent = lax.dot_general(
        spread,
        jnp.concatenate([tokens, cotangent]).astype(F32),
        (((0,), (0,)), ((), ())),
        precision=lax.Precision.HIGHEST,
    ).astype(BF16)
    sent, w_gate, w_up, w_down = lax.optimization_barrier((sent, w_gate, w_up, w_down))
    arrived = exchange(sent.reshape(experts, 2 * CAP, width), "expert")

    weights = jnp.concatenate([w_gate[0], w_up[0], w_down[0]]).reshape(3 * units, high, wide, width)
    weights = jnp.stack(
        swap(lambda m: lax.dynamic_index_in_dim(weights, m, 2, keepdims=False), "col")
    )
    arrived, weights = lax.optimization_barrier((arrived, weights))
    weights_in, weights_out = weights[:, : 2 * units], weights[:, 2 * units :]

    split = jnp.stack([arrived[:, :CAP].reshape(rows, width), arrived[:, CAP:].reshape(rows, width)])
    gathered = share(split, "row")
    inputs, grad_rows = gathered[:, 0], gathered[:, 1]

    partial = jnp.concatenate(
        [
            product(weights_in, inputs, "shyf,yrf->shr").astype(BF16),
            product(weights_out, grad_rows, "shyf,yrf->shr").astype(BF16),
        ],
        axis=1,
    )
    summed = jnp.sum(exchange(partial, "col").astype(F32), axis=0)
    gate_pre, up_pre, hidden_grad = summed[:units], summed[units : 2 * units], summed[2 * units :]
    sigmoid = jax.nn.sigmoid(gate_pre)
    active = gate_pre * sigmoid
    slope = sigmoid * (1.0 + gate_pre * (1.0 - sigmoid))
    mine = jnp.concatenate([hidden_grad * up_pre * slope, hidden_grad * active, active * up_pre]).astype(BF16)
    whole = share(mine, "col")
    deltas, hidden = whole[:, : 2 * units], whole[:, 2 * units :]

    results = jnp.stack(
        [
            product(hidden, weights_out, "shr,shyf->yrf").astype(BF16),
            product(deltas, weights_in, "shr,shyf->yrf").astype(BF16),
        ],
        axis=1,
    )
    results = jnp.sum(exchange(results, "row").astype(F32), axis=0).astype(BF16)
    returned = jnp.concatenate(
        [results[0].reshape(experts, CAP, width), results[1].reshape(experts, CAP, width)], axis=1
    )
    returned, deltas, hidden = lax.optimization_barrier((returned, deltas, hidden))
    returned = exchange(returned, "expert").reshape(2 * rows, width)

    grads = jnp.concatenate(
        [
            product(deltas, inputs, "shr,yrf->shyf").astype(BF16),
            product(hidden, grad_rows, "shr,yrf->shyf").astype(BF16),
        ],
        axis=1,
    )
    grads = jnp.stack(swap(lambda m: lax.dynamic_index_in_dim(grads, m, 0, keepdims=False), "col"), axis=2)
    grads = grads.reshape(3 * units, high * wide * width)
    returned, grads = lax.optimization_barrier((returned, grads))

    mixed = jnp.dot(blend, returned.astype(F32), precision=lax.Precision.HIGHEST).astype(BF16)
    return (
        mixed[:count],
        mixed[count:],
        grads[None, :units],
        grads[None, units : 2 * units],
        grads[None, 2 * units :],
    )


def solution(mesh):
    experts, groups = mesh.devices.shape
    high = max(n for n in range(1, math.isqrt(groups) + 1) if groups % n == 0)
    grid = Mesh(mesh.devices.reshape(experts, high, groups // high), ("expert", "row", "col"))
    by_row, by_hidden = P("expert", ("row", "col")), P("expert", ("row", "col"), None)
    return jax.shard_map(
        shards,
        mesh=grid,
        in_specs=(by_row, P("expert", None), P("expert", None), by_row, by_hidden, by_hidden, by_hidden),
        out_specs=(by_row, by_row, by_hidden, by_hidden, by_hidden),
        check_vma=False,
    )
```

```python
import math

import jax
import jax.numpy as jnp
from jax import lax
from jax.sharding import Mesh, PartitionSpec as P

CAP = 4
F32, BF16 = jnp.float32, jnp.bfloat16


def exchange(values, axis):
    return lax.all_to_all(values, axis, split_axis=0, concat_axis=0, tiled=True)


def share(values, axis):
    copies = jnp.broadcast_to(values[None], (lax.axis_size(axis),) + values.shape)
    return exchange(lax.optimization_barrier(copies), axis)


def product(a, b, pattern):
    return jnp.einsum(pattern, a, b, preferred_element_type=F32)


def swap(block_for, axis):
    size, me = lax.axis_size(axis), lax.axis_index(axis)
    moved = [block_for(me)]
    for shift in range(1, size):
        pairs = [(m, (m + shift) % size) for m in range(size)]
        moved.append(lax.ppermute(block_for((me + shift) % size), axis, pairs))
    ordered = []
    for m in range(size):
        shift = (me - m) % size
        block = moved[0]
        for other in range(1, size):
            block = jnp.where(shift == other, moved[other], block)
        ordered.append(block)
    return ordered


def slot_weights(routes, gates, experts):
    count = routes.shape[0]
    column = lax.broadcasted_iota(jnp.int32, (1, 1, experts * 2 * CAP), 2)
    chosen = routes[:, :, None] == column // (2 * CAP)
    named = jnp.sum(chosen.astype(F32), axis=1)
    weight = jnp.sum(jnp.where(chosen, gates[:, :, None], 0.0), axis=1)
    row = lax.broadcasted_iota(jnp.int32, (count, count), 0)
    before = (lax.broadcasted_iota(jnp.int32, (count, count), 1) < row).astype(BF16)
    position = jnp.dot(before, named.astype(BF16), preferred_element_type=F32).astype(jnp.int32)
    place = column[0] % (2 * CAP)
    first = named * (position == place)
    second = named * (position + CAP == place) * weight
    return jnp.concatenate([first, second]), jnp.concatenate([first * weight, second])


def shards(tokens, routes, gates, cotangent, w_gate, w_up, w_down):
    experts, high, wide = lax.axis_size("expert"), lax.axis_size("row"), lax.axis_size("col")
    count, width = tokens.shape
    units = w_gate.shape[1]
    rows = experts * CAP

    spread, blend = slot_weights(routes, gates, experts)
    sent = lax.dot_general(
        spread,
        jnp.concatenate([tokens, cotangent]).astype(F32),
        (((0,), (0,)), ((), ())),
        precision=lax.Precision.HIGHEST,
    ).astype(BF16)
    sent, w_gate, w_up, w_down = lax.optimization_barrier((sent, w_gate, w_up, w_down))
    arrived = exchange(sent.reshape(experts, 2 * CAP, width), "expert")

    weights = jnp.concatenate([w_gate[0], w_up[0], w_down[0]]).reshape(3 * units, high, wide, width)
    weights = jnp.stack(
        swap(lambda m: lax.dynamic_index_in_dim(weights, m, 2, keepdims=False), "col")
    )
    arrived, weights = lax.optimization_barrier((arrived, weights))
    weights_in, weights_out = weights[:, : 2 * units], weights[:, 2 * units :]

    split = jnp.stack([arrived[:, :CAP].reshape(rows, width), arrived[:, CAP:].reshape(rows, width)])
    gathered = share(split, "row")
    inputs, grad_rows = gathered[:, 0], gathered[:, 1]

    partial = jnp.concatenate(
        [
            product(weights_in, inputs, "shyf,yrf->shr").astype(BF16),
            product(weights_out, grad_rows, "shyf,yrf->shr").astype(BF16),
        ],
        axis=1,
    )
    summed = jnp.sum(share(partial, "col").astype(F32), axis=0)
    gate_pre, up_pre, hidden_grad = summed[:, :units], summed[:, units : 2 * units], summed[:, 2 * units :]
    sigmoid = jax.nn.sigmoid(gate_pre)
    active = gate_pre * sigmoid
    slope = sigmoid * (1.0 + gate_pre * (1.0 - sigmoid))
    deltas = jnp.concatenate([hidden_grad * up_pre * slope, hidden_grad * active], axis=1).astype(BF16)
    hidden = (active * up_pre).astype(BF16)

    results = jnp.stack(
        [
            product(hidden, weights_out, "shr,shyf->yrf").astype(BF16),
            product(deltas, weights_in, "shr,shyf->yrf").astype(BF16),
        ],
        axis=1,
    )
    results = jnp.sum(exchange(results, "row").astype(F32), axis=0).astype(BF16)
    returned = jnp.concatenate(
        [results[0].reshape(experts, CAP, width), results[1].reshape(experts, CAP, width)], axis=1
    )
    returned, deltas, hidden = lax.optimization_barrier((returned, deltas, hidden))
    returned = exchange(returned, "expert").reshape(2 * rows, width)

    grads = jnp.concatenate(
        [
            product(deltas, inputs, "shr,yrf->shyf").astype(BF16),
            product(hidden, grad_rows, "shr,yrf->shyf").astype(BF16),
        ],
        axis=1,
    )
    grads = jnp.stack(swap(lambda m: lax.dynamic_index_in_dim(grads, m, 0, keepdims=False), "col"), axis=2)
    grads = grads.reshape(3, 1, units, high * wide * width)
    returned, *grads = lax.optimization_barrier((returned, grads[0], grads[1], grads[2]))

    mixed = jnp.dot(blend, returned.astype(F32), precision=lax.Precision.HIGHEST).astype(BF16)
    return (mixed[:count], mixed[count:], *grads)


def solution(mesh):
    experts, groups = mesh.devices.shape
    high = max(n for n in range(1, math.isqrt(groups) + 1) if groups % n == 0)
    grid = Mesh(mesh.devices.reshape(experts, high, groups // high), ("expert", "row", "col"))
    by_row, by_hidden = P("expert", ("row", "col")), P("expert", ("row", "col"), None)
    return jax.shard_map(
        shards,
        mesh=grid,
        in_specs=(by_row, P("expert", None), P("expert", None), by_row, by_hidden, by_hidden, by_hidden),
        out_specs=(by_row, by_row, by_hidden, by_hidden, by_hidden),
        check_vma=False,
    )
```

```python
import math

import jax
import jax.numpy as jnp
from jax import lax
from jax.experimental import pallas as pl
from jax.experimental.pallas import tpu as pltpu
from jax.sharding import Mesh, PartitionSpec as P

CAP = 4
F32, BF16 = jnp.float32, jnp.bfloat16


def exchange(values, axis):
    return lax.all_to_all(values, axis, split_axis=0, concat_axis=0, tiled=True)


def share(values, axis):
    copies = jnp.broadcast_to(values[None], (lax.axis_size(axis),) + values.shape)
    return exchange(lax.optimization_barrier(copies), axis)


def product(a, b, pattern):
    return jnp.einsum(pattern, a, b, preferred_element_type=F32)


def swap(block_for, axis):
    size, me = lax.axis_size(axis), lax.axis_index(axis)
    moved = [block_for(me)]
    for shift in range(1, size):
        pairs = [(m, (m + shift) % size) for m in range(size)]
        moved.append(lax.ppermute(block_for((me + shift) % size), axis, pairs))
    ordered = []
    for m in range(size):
        shift = (me - m) % size
        block = moved[0]
        for other in range(1, size):
            block = jnp.where(shift == other, moved[other], block)
        ordered.append(block)
    return ordered


def slot_weights(routes, gates, experts):
    count = routes.shape[0]
    column = lax.broadcasted_iota(jnp.int32, (1, 1, experts * 2 * CAP), 2)
    chosen = routes[:, :, None] == column // (2 * CAP)
    named = jnp.sum(chosen.astype(F32), axis=1)
    weight = jnp.sum(jnp.where(chosen, gates[:, :, None], 0.0), axis=1)
    row = lax.broadcasted_iota(jnp.int32, (count, count), 0)
    before = (lax.broadcasted_iota(jnp.int32, (count, count), 1) < row).astype(BF16)
    position = jnp.dot(before, named.astype(BF16), preferred_element_type=F32).astype(jnp.int32)
    place = column[0] % (2 * CAP)
    return weight * (position == place), weight * (position + CAP == place)


def to_slots_kernel(routes_ref, gates_ref, tokens_ref, cotangent_ref, sent_ref):
    tops, count = routes_ref.shape
    slots = sent_ref.shape[0]
    listed, weights = (jnp.concatenate([ref[...]] * 4, axis=1) for ref in (routes_ref, gates_ref))
    slot = lax.broadcasted_iota(jnp.int32, (slots, 4 * count), 0)
    column = lax.broadcasted_iota(jnp.int32, (slots, 4 * count), 1)
    expert, place = slot // (2 * CAP), slot % (2 * CAP)
    named = jnp.zeros((slots, 4 * count), F32)
    weight = jnp.zeros((slots, 4 * count), F32)
    for k in range(tops):
        chosen = listed[k : k + 1] == expert
        named = jnp.where(chosen, 1.0, named)
        weight = jnp.where(chosen, weights[k : k + 1], weight)
    earlier = lax.broadcasted_iota(jnp.int32, (4 * count, 4 * count), 0)
    later = lax.broadcasted_iota(jnp.int32, (4 * count, 4 * count), 1)
    before = ((earlier < later) & (earlier // count == later // count)).astype(F32).astype(BF16)
    position = jnp.dot(named.astype(BF16), before, preferred_element_type=F32).astype(jnp.int32)
    section = column // count
    high = weight.astype(BF16).astype(F32)
    middle = (weight - high).astype(BF16).astype(F32)
    low = weight - high - middle
    part = jnp.where(section == 0, 1.0, jnp.where(section == 1, high, jnp.where(section == 2, middle, low)))
    wanted = position + jnp.where(section == 0, 0, CAP)
    spread = jnp.where((named > 0.0) & (wanted == place), part, 0.0).astype(BF16)
    cotangents = cotangent_ref[...].astype(F32)
    sources = jnp.concatenate([tokens_ref[...].astype(F32)] + [cotangents] * 3).astype(BF16)
    sent_ref[...] = jnp.dot(spread, sources, preferred_element_type=F32).astype(BF16)


def to_slots(routes, gates, tokens, cotangent, experts):
    slots, width = experts * 2 * CAP, tokens.shape[1]
    return pl.pallas_call(
        to_slots_kernel,
        out_shape=jax.ShapeDtypeStruct((slots, width), BF16),
        grid=(1,),
        in_specs=[pl.BlockSpec(values.shape, lambda i: (0, 0)) for values in (routes.T, gates.T, tokens, cotangent)],
        out_specs=pl.BlockSpec((slots, width), lambda i: (0, 0)),
        compiler_params=pltpu.CompilerParams(vmem_limit_bytes=16 * 1024 * 1024),
        cost_estimate=pl.CostEstimate(flops=8 * slots * width * tokens.shape[0], bytes_accessed=2 * slots * width, transcendentals=0),
        name="to_slots",
    )(routes.T, gates.T, tokens, cotangent)


def shards(tokens, routes, gates, cotangent, w_gate, w_up, w_down):
    experts, high, wide = lax.axis_size("expert"), lax.axis_size("row"), lax.axis_size("col")
    width = tokens.shape[1]
    units = w_gate.shape[1]
    rows = experts * CAP

    sent = to_slots(routes, gates, tokens, cotangent, experts)
    sent, w_gate, w_up, w_down, routes, gates = lax.optimization_barrier(
        (sent, w_gate, w_up, w_down, routes, gates)
    )
    arrived = exchange(sent.reshape(experts, 2 * CAP, width), "expert")

    weights = jnp.concatenate([w_gate[0], w_up[0], w_down[0]]).reshape(3 * units, high, wide, width)
    weights = jnp.stack(
        swap(lambda m: lax.dynamic_index_in_dim(weights, m, 2, keepdims=False), "col")
    )
    blend = slot_weights(routes, gates, experts)
    arrived, weights, blend = lax.optimization_barrier((arrived, weights, blend))
    weights_in, weights_out = weights[:, : 2 * units], weights[:, 2 * units :]

    split = jnp.stack([arrived[:, :CAP].reshape(rows, width), arrived[:, CAP:].reshape(rows, width)])
    gathered = share(split, "row")
    inputs, grad_rows = gathered[:, 0], gathered[:, 1]

    partial = jnp.concatenate(
        [
            product(weights_in, inputs, "shyf,yrf->shr").astype(BF16),
            product(weights_out, grad_rows, "shyf,yrf->shr").astype(BF16),
        ],
        axis=1,
    )
    summed = jnp.sum(share(partial, "col").astype(F32), axis=0)
    gate_pre, up_pre, hidden_grad = summed[:, :units], summed[:, units : 2 * units], summed[:, 2 * units :]
    sigmoid = jax.nn.sigmoid(gate_pre)
    active = gate_pre * sigmoid
    slope = sigmoid * (1.0 + gate_pre * (1.0 - sigmoid))
    deltas = jnp.concatenate([hidden_grad * up_pre * slope, hidden_grad * active], axis=1).astype(BF16)
    hidden = (active * up_pre).astype(BF16)

    blocks = jnp.concatenate(
        [
            jnp.concatenate([jnp.zeros_like(deltas), hidden], axis=1),
            jnp.concatenate([deltas, jnp.zeros_like(hidden)], axis=1),
        ],
        axis=2,
    )
    results = product(blocks, weights, "shr,shyf->yrf").astype(BF16)
    results = jnp.sum(exchange(results, "row").astype(F32), axis=0).astype(BF16)
    returned = jnp.concatenate(
        [results[:rows].reshape(experts, CAP, width), results[rows:].reshape(experts, CAP, width)], axis=1
    )
    returned, deltas, hidden = lax.optimization_barrier((returned, deltas, hidden))
    returned = exchange(returned, "expert").reshape(2 * rows, width)

    grads = jnp.concatenate(
        [
            product(deltas, inputs, "shr,yrf->shyf").astype(BF16),
            product(hidden, grad_rows, "shr,yrf->shyf").astype(BF16),
        ],
        axis=1,
    )
    grads = jnp.stack(swap(lambda m: lax.dynamic_index_in_dim(grads, m, 0, keepdims=False), "col"), axis=2)
    grads = grads.reshape(3, 1, units, high * wide * width)
    returned, *grads = lax.optimization_barrier((returned, grads[0], grads[1], grads[2]))

    returned = returned.astype(F32)
    mixed, token_grad = (jnp.dot(gate, returned, precision=lax.Precision.HIGHEST).astype(BF16) for gate in blend)
    return (mixed, token_grad, *grads)


def solution(mesh):
    experts, groups = mesh.devices.shape
    high = max(n for n in range(1, math.isqrt(groups) + 1) if groups % n == 0)
    grid = Mesh(mesh.devices.reshape(experts, high, groups // high), ("expert", "row", "col"))
    by_row, by_hidden = P("expert", ("row", "col")), P("expert", ("row", "col"), None)
    return jax.shard_map(
        shards,
        mesh=grid,
        in_specs=(by_row, P("expert", None), P("expert", None), by_row, by_hidden, by_hidden, by_hidden),
        out_specs=(by_row, by_row, by_hidden, by_hidden, by_hidden),
        check_vma=False,
    )
```

```python
import math

import jax
import jax.numpy as jnp
from jax import lax
from jax.experimental import pallas as pl
from jax.sharding import Mesh, PartitionSpec as P

CAP = 4
F32, BF16 = jnp.float32, jnp.bfloat16


def exchange(values, axis):
    return lax.all_to_all(values, axis, split_axis=0, concat_axis=0, tiled=True)


def share(values, axis):
    copies = jnp.broadcast_to(values[None], (lax.axis_size(axis),) + values.shape)
    return exchange(lax.optimization_barrier(copies), axis)


def product(a, b, pattern):
    return jnp.einsum(pattern, a, b, preferred_element_type=F32)


def swap(block_for, axis):
    size, me = lax.axis_size(axis), lax.axis_index(axis)
    moved = [block_for(me)]
    for shift in range(1, size):
        pairs = [(m, (m + shift) % size) for m in range(size)]
        moved.append(lax.ppermute(block_for((me + shift) % size), axis, pairs))
    ordered = []
    for m in range(size):
        shift = (me - m) % size
        block = moved[0]
        for other in range(1, size):
            block = jnp.where(shift == other, moved[other], block)
        ordered.append(block)
    return ordered


def slot_weights(routes, gates, experts):
    count = routes.shape[0]
    column = lax.broadcasted_iota(jnp.int32, (1, 1, experts * 2 * CAP), 2)
    chosen = routes[:, :, None] == column // (2 * CAP)
    named = jnp.sum(chosen.astype(F32), axis=1)
    weight = jnp.sum(jnp.where(chosen, gates[:, :, None], 0.0), axis=1)
    row = lax.broadcasted_iota(jnp.int32, (count, count), 0)
    before = (lax.broadcasted_iota(jnp.int32, (count, count), 1) < row).astype(BF16)
    position = jnp.dot(before, named.astype(BF16), preferred_element_type=F32).astype(jnp.int32)
    place = column[0] % (2 * CAP)
    return jnp.concatenate([weight * (position == place), weight * (position + CAP == place)])


def to_slots_kernel(routes_ref, gates_ref, tokens_ref, cotangent_ref, sent_ref):
    tops, count = routes_ref.shape
    slots = sent_ref.shape[0]
    listed, weights = (jnp.concatenate([ref[...]] * 4, axis=1) for ref in (routes_ref, gates_ref))
    slot = lax.broadcasted_iota(jnp.int32, (slots, 4 * count), 0)
    column = lax.broadcasted_iota(jnp.int32, (slots, 4 * count), 1)
    expert, place = slot // (2 * CAP), slot % (2 * CAP)
    named = jnp.zeros((slots, 4 * count), F32)
    weight = jnp.zeros((slots, 4 * count), F32)
    for k in range(tops):
        chosen = listed[k : k + 1] == expert
        named = jnp.where(chosen, 1.0, named)
        weight = jnp.where(chosen, weights[k : k + 1], weight)
    earlier = lax.broadcasted_iota(jnp.int32, (4 * count, 4 * count), 0)
    later = lax.broadcasted_iota(jnp.int32, (4 * count, 4 * count), 1)
    before = ((earlier < later) & (earlier // count == later // count)).astype(F32).astype(BF16)
    position = jnp.dot(named.astype(BF16), before, preferred_element_type=F32).astype(jnp.int32)
    section = column // count
    high = weight.astype(BF16).astype(F32)
    middle = (weight - high).astype(BF16).astype(F32)
    low = weight - high - middle
    part = jnp.where(section == 0, 1.0, jnp.where(section == 1, high, jnp.where(section == 2, middle, low)))
    wanted = position + jnp.where(section == 0, 0, CAP)
    spread = jnp.where((named > 0.0) & (wanted == place), part, 0.0).astype(BF16)
    cotangents = cotangent_ref[...].astype(F32)
    sources = jnp.concatenate([tokens_ref[...].astype(F32)] + [cotangents] * 3).astype(BF16)
    sent_ref[...] = jnp.dot(spread, sources, preferred_element_type=F32).astype(BF16)


def to_slots(routes, gates, tokens, cotangent, experts):
    slots, width = experts * 2 * CAP, tokens.shape[1]
    return pl.pallas_call(
        to_slots_kernel,
        out_shape=jax.ShapeDtypeStruct((slots, width), BF16),
        grid=(1,),
        in_specs=[pl.BlockSpec(values.shape, lambda i: (0, 0)) for values in (routes.T, gates.T, tokens, cotangent)],
        out_specs=pl.BlockSpec((slots, width), lambda i: (0, 0)),
        cost_estimate=pl.CostEstimate(flops=8 * slots * width * tokens.shape[0], bytes_accessed=2 * slots * width, transcendentals=0),
        name="to_slots",
    )(routes.T, gates.T, tokens, cotangent)


def shards(tokens, routes, gates, cotangent, w_gate, w_up, w_down):
    experts, high, wide = lax.axis_size("expert"), lax.axis_size("row"), lax.axis_size("col")
    width = tokens.shape[1]
    units = w_gate.shape[1]
    rows = experts * CAP

    sent = to_slots(routes, gates, tokens, cotangent, experts)
    sent, w_gate, w_up, w_down, routes, gates = lax.optimization_barrier(
        (sent, w_gate, w_up, w_down, routes, gates)
    )
    arrived = exchange(sent.reshape(experts, 2 * CAP, width), "expert")

    weights = jnp.concatenate([w_gate[0], w_up[0], w_down[0]]).reshape(3 * units, high, wide, width)
    weights = jnp.stack(
        swap(lambda m: lax.dynamic_index_in_dim(weights, m, 2, keepdims=False), "col")
    )
    blend = slot_weights(routes, gates, experts)
    arrived, weights, blend = lax.optimization_barrier((arrived, weights, blend))
    weights_in, weights_out = weights[:, : 2 * units], weights[:, 2 * units :]

    split = jnp.stack([arrived[:, :CAP].reshape(rows, width), arrived[:, CAP:].reshape(rows, width)])
    gathered = share(split, "row")
    inputs, grad_rows = gathered[:, 0], gathered[:, 1]

    partial = jnp.concatenate(
        [
            product(weights_in, inputs, "shyf,yrf->shr").astype(BF16),
            product(weights_out, grad_rows, "shyf,yrf->shr").astype(BF16),
        ],
        axis=1,
    )
    summed = jnp.sum(share(partial, "col").astype(F32), axis=0)
    gate_pre, up_pre, hidden_grad = summed[:, :units], summed[:, units : 2 * units], summed[:, 2 * units :]
    sigmoid = jax.nn.sigmoid(gate_pre)
    active = gate_pre * sigmoid
    slope = sigmoid * (1.0 + gate_pre * (1.0 - sigmoid))
    deltas = jnp.concatenate([hidden_grad * up_pre * slope, hidden_grad * active], axis=1).astype(BF16)
    hidden = (active * up_pre).astype(BF16)

    blocks = jnp.concatenate(
        [
            jnp.concatenate([jnp.zeros_like(deltas), hidden], axis=1),
            jnp.concatenate([deltas, jnp.zeros_like(hidden)], axis=1),
        ],
        axis=2,
    )
    results = product(blocks, weights, "shr,shyf->yrf").astype(BF16)
    results = jnp.sum(exchange(results, "row").astype(F32), axis=0).astype(BF16)
    returned = jnp.concatenate(
        [results[:rows].reshape(experts, CAP, width), results[rows:].reshape(experts, CAP, width)], axis=1
    )
    returned, deltas, hidden = lax.optimization_barrier((returned, deltas, hidden))
    returned = exchange(returned, "expert").reshape(2 * rows, width)

    grads = jnp.concatenate(
        [
            product(deltas, inputs, "shr,yrf->shyf").astype(BF16),
            product(hidden, grad_rows, "shr,yrf->shyf").astype(BF16),
        ],
        axis=1,
    )
    grads = jnp.stack(swap(lambda m: lax.dynamic_index_in_dim(grads, m, 0, keepdims=False), "col"), axis=2)
    grads = grads.reshape(3, 1, units, high * wide * width)
    returned, *grads = lax.optimization_barrier((returned, grads[0], grads[1], grads[2]))

    mixed = jnp.dot(blend, returned.astype(F32), precision=lax.Precision.HIGHEST).astype(BF16)
    count = tokens.shape[0]
    return (mixed[:count], mixed[count:], *grads)


def solution(mesh):
    experts, groups = mesh.devices.shape
    high = max(n for n in range(1, math.isqrt(groups) + 1) if groups % n == 0)
    grid = Mesh(mesh.devices.reshape(experts, high, groups // high), ("expert", "row", "col"))
    by_row, by_hidden = P("expert", ("row", "col")), P("expert", ("row", "col"), None)
    return jax.shard_map(
        shards,
        mesh=grid,
        in_specs=(by_row, P("expert", None), P("expert", None), by_row, by_hidden, by_hidden, by_hidden),
        out_specs=(by_row, by_row, by_hidden, by_hidden, by_hidden),
        check_vma=False,
    )
```

```python
import math

import jax
import jax.numpy as jnp
from jax import lax
from jax.experimental import pallas as pl
from jax.sharding import Mesh, PartitionSpec as P

CAP = 4
F32, BF16 = jnp.float32, jnp.bfloat16


def exchange(values, axis):
    return lax.all_to_all(values, axis, split_axis=0, concat_axis=0, tiled=True)


def share(values, axis):
    copies = jnp.broadcast_to(values[None], (lax.axis_size(axis),) + values.shape)
    return exchange(lax.optimization_barrier(copies), axis)


def product(a, b, pattern):
    return jnp.einsum(pattern, a, b, preferred_element_type=F32)


def swap(block_for, axis):
    size, me = lax.axis_size(axis), lax.axis_index(axis)
    moved = [block_for(me)]
    for shift in range(1, size):
        pairs = [(m, (m + shift) % size) for m in range(size)]
        moved.append(lax.ppermute(block_for((me + shift) % size), axis, pairs))
    ordered = []
    for m in range(size):
        shift = (me - m) % size
        block = moved[0]
        for other in range(1, size):
            block = jnp.where(shift == other, moved[other], block)
        ordered.append(block)
    return ordered


def slot_weights(routes, gates, experts):
    count = routes.shape[0]
    column = lax.broadcasted_iota(jnp.int32, (1, 1, experts * 2 * CAP), 2)
    chosen = routes[:, :, None] == column // (2 * CAP)
    named = jnp.sum(chosen.astype(F32), axis=1)
    weight = jnp.sum(jnp.where(chosen, gates[:, :, None], 0.0), axis=1)
    row = lax.broadcasted_iota(jnp.int32, (count, count), 0)
    before = (lax.broadcasted_iota(jnp.int32, (count, count), 1) < row).astype(BF16)
    position = jnp.dot(before, named.astype(BF16), preferred_element_type=F32).astype(jnp.int32)
    place = column[0] % (2 * CAP)
    return jnp.concatenate([weight * (position == place), weight * (position + CAP == place)])


def to_slots_kernel(routes_ref, gates_ref, tokens_ref, cotangent_ref, sent_ref):
    tops, count = routes_ref.shape
    slots = sent_ref.shape[0]
    experts = slots // (2 * CAP)
    listed, weights = (jnp.concatenate([ref[...]] * 4, axis=1) for ref in (routes_ref, gates_ref))
    expert = lax.broadcasted_iota(jnp.int32, (experts, 4 * count), 0)
    section = lax.broadcasted_iota(jnp.int32, (experts, 4 * count), 1) // count
    named = jnp.zeros((experts, 4 * count), F32)
    weight = jnp.zeros((experts, 4 * count), F32)
    for k in range(tops):
        chosen = listed[k : k + 1] == expert
        named = jnp.where(chosen, 1.0, named)
        weight = jnp.where(chosen, weights[k : k + 1], weight)
    earlier = lax.broadcasted_iota(jnp.int32, (4 * count, 4 * count), 0)
    later = lax.broadcasted_iota(jnp.int32, (4 * count, 4 * count), 1)
    before = ((earlier < later) & (earlier // count == later // count)).astype(F32).astype(BF16)
    position = jnp.dot(named.astype(BF16), before, preferred_element_type=F32).astype(jnp.int32)
    high = weight.astype(BF16).astype(F32)
    middle = (weight - high).astype(BF16).astype(F32)
    low = weight - high - middle
    part = jnp.where(section == 0, named, jnp.where(section == 1, high, jnp.where(section == 2, middle, low)))
    wanted = position + jnp.where(section == 0, 0, CAP)

    def over_slots(values):
        return jnp.broadcast_to(values[:, None], (experts, 2 * CAP, 4 * count)).reshape(slots, 4 * count)

    place = lax.broadcasted_iota(jnp.int32, (slots, 4 * count), 0) % (2 * CAP)
    spread = jnp.where(over_slots(wanted) == place, over_slots(part), 0.0).astype(BF16)
    cotangents = cotangent_ref[...].astype(F32)
    sources = jnp.concatenate([tokens_ref[...].astype(F32)] + [cotangents] * 3).astype(BF16)
    sent_ref[...] = jnp.dot(spread, sources, preferred_element_type=F32).astype(BF16)


def to_slots(routes, gates, tokens, cotangent, experts):
    slots, width = experts * 2 * CAP, tokens.shape[1]
    return pl.pallas_call(
        to_slots_kernel,
        out_shape=jax.ShapeDtypeStruct((slots, width), BF16),
        grid=(1,),
        in_specs=[pl.BlockSpec(values.shape, lambda i: (0, 0)) for values in (routes.T, gates.T, tokens, cotangent)],
        out_specs=pl.BlockSpec((slots, width), lambda i: (0, 0)),
        cost_estimate=pl.CostEstimate(flops=8 * slots * width * tokens.shape[0], bytes_accessed=2 * slots * width, transcendentals=0),
        name="to_slots",
    )(routes.T, gates.T, tokens, cotangent)


def shards(tokens, routes, gates, cotangent, w_gate, w_up, w_down):
    experts, high, wide = lax.axis_size("expert"), lax.axis_size("row"), lax.axis_size("col")
    width = tokens.shape[1]
    units = w_gate.shape[1]
    rows = experts * CAP

    sent = to_slots(routes, gates, tokens, cotangent, experts)
    sent, w_gate, w_up, w_down, routes, gates = lax.optimization_barrier(
        (sent, w_gate, w_up, w_down, routes, gates)
    )
    arrived = exchange(sent.reshape(experts, 2 * CAP, width), "expert")

    weights = jnp.concatenate([w_gate[0], w_up[0], w_down[0]]).reshape(3 * units, high, wide, width)
    weights = jnp.stack(
        swap(lambda m: lax.dynamic_index_in_dim(weights, m, 2, keepdims=False), "col")
    )
    blend = slot_weights(routes, gates, experts)
    arrived, weights, blend = lax.optimization_barrier((arrived, weights, blend))
    weights_in, weights_out = weights[:, : 2 * units], weights[:, 2 * units :]

    split = jnp.stack([arrived[:, :CAP].reshape(rows, width), arrived[:, CAP:].reshape(rows, width)])
    gathered = share(split, "row")
    inputs, grad_rows = gathered[:, 0], gathered[:, 1]

    partial = jnp.concatenate(
        [
            product(weights_in, inputs, "shyf,yrf->shr").astype(BF16),
            product(weights_out, grad_rows, "shyf,yrf->shr").astype(BF16),
        ],
        axis=1,
    )
    summed = jnp.sum(share(partial, "col").astype(F32), axis=0)
    gate_pre, up_pre, hidden_grad = summed[:, :units], summed[:, units : 2 * units], summed[:, 2 * units :]
    sigmoid = jax.nn.sigmoid(gate_pre)
    active = gate_pre * sigmoid
    slope = sigmoid * (1.0 + gate_pre * (1.0 - sigmoid))
    deltas = jnp.concatenate([hidden_grad * up_pre * slope, hidden_grad * active], axis=1).astype(BF16)
    hidden = (active * up_pre).astype(BF16)

    blocks = jnp.concatenate(
        [
            jnp.concatenate([jnp.zeros_like(deltas), hidden], axis=1),
            jnp.concatenate([deltas, jnp.zeros_like(hidden)], axis=1),
        ],
        axis=2,
    )
    results = product(blocks, weights, "shr,shyf->ryf").astype(BF16).swapaxes(0, 1)
    results = jnp.sum(exchange(results, "row").astype(F32), axis=0).astype(BF16)
    returned = jnp.concatenate(
        [results[:rows].reshape(experts, CAP, width), results[rows:].reshape(experts, CAP, width)], axis=1
    )
    returned, deltas, hidden = lax.optimization_barrier((returned, deltas, hidden))
    returned = exchange(returned, "expert").reshape(2 * rows, width)

    grads = jnp.concatenate(
        [
            product(deltas, inputs, "shr,yrf->shyf").astype(BF16),
            product(hidden, grad_rows, "shr,yrf->shyf").astype(BF16),
        ],
        axis=1,
    )
    grads = jnp.stack(swap(lambda m: lax.dynamic_index_in_dim(grads, m, 0, keepdims=False), "col"), axis=2)
    grads = grads.reshape(3, 1, units, high * wide * width)
    returned, *grads = lax.optimization_barrier((returned, grads[0], grads[1], grads[2]))

    mixed = jnp.dot(blend, returned.astype(F32), precision=lax.Precision.HIGHEST).astype(BF16)
    count = tokens.shape[0]
    return (mixed[:count], mixed[count:], *grads)


def solution(mesh):
    experts, groups = mesh.devices.shape
    high = max(n for n in range(1, math.isqrt(groups) + 1) if groups % n == 0)
    grid = Mesh(mesh.devices.reshape(experts, high, groups // high), ("expert", "row", "col"))
    by_row, by_hidden = P("expert", ("row", "col")), P("expert", ("row", "col"), None)
    return jax.shard_map(
        shards,
        mesh=grid,
        in_specs=(by_row, P("expert", None), P("expert", None), by_row, by_hidden, by_hidden, by_hidden),
        out_specs=(by_row, by_row, by_hidden, by_hidden, by_hidden),
        check_vma=False,
    )
```

```python
import math

import jax
import jax.numpy as jnp
from jax import lax
from jax.experimental import pallas as pl
from jax.sharding import Mesh, PartitionSpec as P

CAP = 4
F32, BF16 = jnp.float32, jnp.bfloat16


def exchange(values, axis):
    return lax.all_to_all(values, axis, split_axis=0, concat_axis=0, tiled=True)


def share(values, axis):
    copies = jnp.broadcast_to(values[None], (lax.axis_size(axis),) + values.shape)
    return exchange(lax.optimization_barrier(copies), axis)


def product(a, b, pattern):
    return jnp.einsum(pattern, a, b, preferred_element_type=F32)


def swap(block_for, axis):
    size, me = lax.axis_size(axis), lax.axis_index(axis)
    moved = [block_for(me)]
    for shift in range(1, size):
        pairs = [(m, (m + shift) % size) for m in range(size)]
        moved.append(lax.ppermute(block_for((me + shift) % size), axis, pairs))
    ordered = []
    for m in range(size):
        shift = (me - m) % size
        block = moved[0]
        for other in range(1, size):
            block = jnp.where(shift == other, moved[other], block)
        ordered.append(block)
    return ordered


def slot_weights(routes, gates, experts):
    count = routes.shape[0]
    column = lax.broadcasted_iota(jnp.int32, (1, 1, experts * 2 * CAP), 2)
    chosen = routes[:, :, None] == column // (2 * CAP)
    named = jnp.sum(chosen.astype(F32), axis=1)
    weight = jnp.sum(jnp.where(chosen, gates[:, :, None], 0.0), axis=1)
    row = lax.broadcasted_iota(jnp.int32, (count, count), 0)
    before = (lax.broadcasted_iota(jnp.int32, (count, count), 1) < row).astype(BF16)
    position = jnp.dot(before, named.astype(BF16), preferred_element_type=F32).astype(jnp.int32)
    place = column[0] % (2 * CAP)
    return jnp.concatenate([weight * (position == place), weight * (position + CAP == place)])


def to_slots_kernel(routes_ref, gates_ref, tokens_ref, cotangent_ref, sent_ref):
    tops, count = routes_ref.shape
    slots = sent_ref.shape[0]
    experts = slots // (2 * CAP)
    listed, weights = (jnp.concatenate([ref[...]] * 4, axis=1) for ref in (routes_ref, gates_ref))
    expert = lax.broadcasted_iota(jnp.int32, (experts, 4 * count), 0)
    section = lax.broadcasted_iota(jnp.int32, (experts, 4 * count), 1) // count
    named = jnp.zeros((experts, 4 * count), F32)
    weight = jnp.zeros((experts, 4 * count), F32)
    for k in range(tops):
        chosen = listed[k : k + 1] == expert
        named = jnp.where(chosen, 1.0, named)
        weight = jnp.where(chosen, weights[k : k + 1], weight)
    earlier = lax.broadcasted_iota(jnp.int32, (4 * count, 4 * count), 0)
    later = lax.broadcasted_iota(jnp.int32, (4 * count, 4 * count), 1)
    before = ((earlier < later) & (earlier // count == later // count)).astype(F32).astype(BF16)
    position = jnp.dot(named.astype(BF16), before, preferred_element_type=F32).astype(jnp.int32)
    high = weight.astype(BF16).astype(F32)
    middle = (weight - high).astype(BF16).astype(F32)
    low = weight - high - middle
    part = jnp.where(section == 0, named, jnp.where(section == 1, high, jnp.where(section == 2, middle, low)))
    wanted = position + jnp.where(section == 0, 0, CAP)

    def over_slots(values):
        return jnp.broadcast_to(values[:, None], (experts, 2 * CAP, 4 * count)).reshape(slots, 4 * count)

    place = lax.broadcasted_iota(jnp.int32, (slots, 4 * count), 0) % (2 * CAP)
    spread = jnp.where(over_slots(wanted) == place, over_slots(part), 0.0).astype(BF16)
    cotangents = cotangent_ref[...].astype(F32)
    sources = jnp.concatenate([tokens_ref[...].astype(F32)] + [cotangents] * 3).astype(BF16)
    sent_ref[...] = jnp.dot(spread, sources, preferred_element_type=F32).astype(BF16)


def to_slots(routes, gates, tokens, cotangent, experts):
    slots, width = experts * 2 * CAP, tokens.shape[1]
    return pl.pallas_call(
        to_slots_kernel,
        out_shape=jax.ShapeDtypeStruct((slots, width), BF16),
        grid=(1,),
        in_specs=[pl.BlockSpec(values.shape, lambda i: (0, 0)) for values in (routes.T, gates.T, tokens, cotangent)],
        out_specs=pl.BlockSpec((slots, width), lambda i: (0, 0)),
        cost_estimate=pl.CostEstimate(flops=8 * slots * width * tokens.shape[0], bytes_accessed=2 * slots * width, transcendentals=0),
        name="to_slots",
    )(routes.T, gates.T, tokens, cotangent)


def shards(tokens, routes, gates, cotangent, w_gate, w_up, w_down):
    experts, high, wide = lax.axis_size("expert"), lax.axis_size("row"), lax.axis_size("col")
    width = tokens.shape[1]
    units = w_gate.shape[1]
    rows = experts * CAP

    sent = to_slots(routes, gates, tokens, cotangent, experts)
    sent, w_gate, w_up, w_down, routes, gates = lax.optimization_barrier(
        (sent, w_gate, w_up, w_down, routes, gates)
    )
    arrived = exchange(sent.reshape(experts, 2 * CAP, width), "expert")

    weights = jnp.concatenate([w_gate[0], w_up[0], w_down[0]]).reshape(3 * units, high, wide, width)
    weights = jnp.stack(
        swap(lambda m: lax.dynamic_index_in_dim(weights, m, 2, keepdims=False), "col")
    )
    blend = slot_weights(routes, gates, experts)
    arrived, weights, blend = lax.optimization_barrier((arrived, weights, blend))
    weights_in, weights_out = weights[:, : 2 * units], weights[:, 2 * units :]

    split = jnp.stack([arrived[:, :CAP].reshape(rows, width), arrived[:, CAP:].reshape(rows, width)])
    gathered = share(split, "row")
    inputs, grad_rows = gathered[:, 0], gathered[:, 1]

    partial = jnp.concatenate(
        [
            product(weights_in, inputs, "shyf,yrf->shr").astype(BF16),
            product(weights_out, grad_rows, "shyf,yrf->shr").astype(BF16),
        ],
        axis=1,
    )
    summed = jnp.sum(exchange(partial, "col").astype(F32), axis=0)
    gate_pre, up_pre, hidden_grad = summed[:units], summed[units : 2 * units], summed[2 * units :]
    sigmoid = jax.nn.sigmoid(gate_pre)
    active = gate_pre * sigmoid
    slope = sigmoid * (1.0 + gate_pre * (1.0 - sigmoid))
    mine = jnp.concatenate([hidden_grad * up_pre * slope, hidden_grad * active, active * up_pre]).astype(BF16)
    whole = share(mine, "col")
    deltas, hidden = whole[:, : 2 * units], whole[:, 2 * units :]

    blocks = jnp.concatenate(
        [
            jnp.concatenate([jnp.zeros_like(deltas), hidden], axis=1),
            jnp.concatenate([deltas, jnp.zeros_like(hidden)], axis=1),
        ],
        axis=2,
    )
    results = product(blocks, weights, "shr,shyf->ryf").astype(BF16).swapaxes(0, 1)
    results = jnp.sum(exchange(results, "row").astype(F32), axis=0).astype(BF16)
    returned = jnp.concatenate(
        [results[:rows].reshape(experts, CAP, width), results[rows:].reshape(experts, CAP, width)], axis=1
    )
    returned, deltas, hidden = lax.optimization_barrier((returned, deltas, hidden))
    returned = exchange(returned, "expert").reshape(2 * rows, width)

    grads = jnp.concatenate(
        [
            product(deltas, inputs, "shr,yrf->shyf").astype(BF16),
            product(hidden, grad_rows, "shr,yrf->shyf").astype(BF16),
        ],
        axis=1,
    )
    grads = jnp.stack(swap(lambda m: lax.dynamic_index_in_dim(grads, m, 0, keepdims=False), "col"), axis=2)
    grads = grads.reshape(3, 1, units, high * wide * width)
    returned, *grads = lax.optimization_barrier((returned, grads[0], grads[1], grads[2]))

    mixed = jnp.dot(blend, returned.astype(F32), precision=lax.Precision.HIGHEST).astype(BF16)
    count = tokens.shape[0]
    return (mixed[:count], mixed[count:], *grads)


def solution(mesh):
    experts, groups = mesh.devices.shape
    high = max(n for n in range(1, math.isqrt(groups) + 1) if groups % n == 0)
    grid = Mesh(mesh.devices.reshape(experts, high, groups // high), ("expert", "row", "col"))
    by_row, by_hidden = P("expert", ("row", "col")), P("expert", ("row", "col"), None)
    return jax.shard_map(
        shards,
        mesh=grid,
        in_specs=(by_row, P("expert", None), P("expert", None), by_row, by_hidden, by_hidden, by_hidden),
        out_specs=(by_row, by_row, by_hidden, by_hidden, by_hidden),
        check_vma=False,
    )
```
